256 devices in a mesh: grid: 64 (over z, y, core), rep: 4 (over x).
Axes of the slice: x: 4, y: 4, z: 8, core: 2. Of those that a mesh axis runs over, the one named last changes fastest.
Arguments:
- amplitudes: bfloat16 [22016, 4, 3072], P(None, 'rep', 'grid'), may hold values from -6 to 6
- integrals: bfloat16 [2048, 4, 3072], P(None, 'rep'), may hold values from -0.0546875 to 0.0546875
- rest_terms: bfloat16 [2048, 22016], P(('grid', 'rep')), may hold values from -6 to 6
- occupied_energy: float32 [150], replicated, may hold values from -1.5 to -0.3
- virtual_energy: float32 [900], replicated, may hold values from 0.1 to 3
- slab_start: int32 [1], replicated, may hold values from 0 to 807952
Outputs:
- new_amplitudes: bfloat16 [2048, 22016], P(('grid', 'rep'))
The draws below stay inside these ranges and needn't reach their ends.
Inputs may be any that keep to these rules, and one draw needn't show every extreme that they name: `slab_start`: the slab lies within the 810000 virtual pairs.
All inputs are finite; a program needn't handle non-finite values.
Results may differ from the reference program's by a relative error of at most 0.0039.
Values may be sent and summed in bfloat16 or wider, within the bound.
No kernel may reach another device: no remote copies, remote signals or barrier semaphores. Data moves between devices by JAX's collectives and lax.ppermute only.
A program may use at most 128 MiB of HBM per device.

```python
import jax
import jax.numpy as jnp
from jax import lax

O = 150
V = 900
IJ = 22016
CD = 12288
Q = 2048
REPS = 4
CD_REP = 3072


def shard_levels(key, shape, pieces, smallest, top_value):
    factor_of, own = 1.0, jax.random.fold_in(key, 6)
    for axis_at, shards_of in pieces:
        heights = jnp.exp(jax.random.uniform(jax.random.fold_in(own, axis_at), (shards_of,), jnp.float32, smallest / len(pieces), top_value / len(pieces)))
        factor_of = factor_of * jnp.repeat(heights, shape[axis_at] // shards_of).reshape([-1 if axis == axis_at else 1 for axis in range(len(shape))])
    return factor_of


def noise(key, shape, spread, reach, shards=(), kind=jnp.bfloat16):
    array = jax.random.normal(key, shape, jnp.float32) * spread
    if len(shards) > 0:
        array = shard_levels(key, shape, shards, -0.22, 0.18) * array
    return jnp.clip(array, min=-reach, max=reach).astype(kind)


def setup_inputs(seed: int = 0) -> dict:
    streams_of = jax.random.split(jax.random.key(seed), 7)
    return {
        "amplitudes": noise(streams_of[0], (IJ, REPS, CD_REP), 1.0, 6.0, ((1, 4), (2, 64))),
        "integrals": noise(streams_of[1], (Q, REPS, CD_REP), CD ** -0.5, 0.0546875, ((1, 4),)),
        "rest_terms": noise(streams_of[2], (Q, IJ), 1.0, 6.0, ((0, 256),)),
        "occupied_energy": jnp.clip(jax.random.uniform(streams_of[3], (O,), jnp.float32, -1.5, -0.3), -1.5, -0.3),
        "virtual_energy": jnp.clip(jax.random.uniform(streams_of[4], (V,), jnp.float32, 0.1, 3.0), 0.1, 3.0),
        "slab_start": jax.random.randint(streams_of[5], (1,), 0, V * V - Q + 1).astype(jnp.int32),
    }


def reference(amplitudes, integrals, rest_terms, occupied_energy, virtual_energy, slab_start):
    amplitude_rows = amplitudes.reshape(IJ, CD)
    integral_rows = integrals.reshape(Q, CD)
    ladder = lax.dot_general(integral_rows, amplitude_rows, (((1,), (1,)), ((), ())), preferred_element_type=jnp.float32).astype(jnp.bfloat16)
    occupied_sum = (occupied_energy[:, None] + occupied_energy[None, :]).reshape(O * O)[:IJ]
    pair_index = slab_start[0] + jnp.arange(Q, dtype=jnp.int32)
    first_orbital = pair_index // V
    second_orbital = pair_index % V
    virtual_sum = virtual_energy[first_orbital] + virtual_energy[second_orbital]
    denominator = occupied_sum[None, :] - virtual_sum[:, None]
    updated = (ladder.astype(jnp.float32) + rest_terms.astype(jnp.float32)) / denominator
    return updated.astype(jnp.bfloat16)
```

```python
import functools

import jax
import jax.numpy as jnp
from jax import lax
from jax.experimental import pallas as pl
from jax.experimental.pallas import tpu as pltpu
from jax.sharding import Mesh, PartitionSpec as P

Z, Y, CORES, REPS = 8, 4, 2, 4
CHIPS = Z * Y
TILE = 128
BF16, F32 = jnp.bfloat16, jnp.float32


def tile_starts(tiles, width):
    return [min(tiles * h // CHIPS, tiles - width) for h in range(CHIPS)]


def repack_kernel(starts, lanes, amp_ref, out_ref, sem):
    copies = [
        pltpu.make_async_copy(
            amp_ref.at[:, pl.ds(start * TILE, lanes)], out_ref.at[h], sem.at[h]
        )
        for h, start in enumerate(starts)
    ]
    for copy in copies:
        copy.start()
    for copy in copies:
        copy.wait()


def repack(amp, starts, lanes):
    return pl.pallas_call(
        functools.partial(repack_kernel, starts, lanes),
        out_shape=jax.ShapeDtypeStruct((CHIPS, amp.shape[0], lanes), amp.dtype),
        in_specs=[pl.BlockSpec(memory_space=pl.ANY)],
        out_specs=pl.BlockSpec(memory_space=pl.ANY),
        scratch_shapes=[pltpu.SemaphoreType.DMA((CHIPS,))],
    )(amp)


def matmul_kernel(
    place_ref, own_ref, other_ref, weight_ref, keep_ref, to1_ref, to2_ref, to3_ref, rows, total, sem
):
    core, rep = place_ref[0], place_ref[1]
    step = pl.program_id(0)

    @pl.when(step == 0)
    def _():
        first = pltpu.make_async_copy(own_ref, rows.at[:, core], sem.at[0])
        second = pltpu.make_async_copy(other_ref, rows.at[:, 1 - core], sem.at[1])
        first.start()
        second.start()
        first.wait()
        second.wait()

    lanes = total.shape[-1]
    depth = weight_ref.shape[-1]
    height = weight_ref.shape[0] * weight_ref.shape[2]
    weight = weight_ref[...].reshape(height, depth)
    for start in range(0, lanes, 256):
        part = rows[:, :, :, start : start + 256].reshape(depth, 256)
        term = jnp.dot(weight, part, preferred_element_type=F32)
        total[:, :, :, start : start + 256] = term.reshape(total.shape[:3] + (256,))
    block = keep_ref.shape
    keep_ref[...] = total[:, rep].reshape(block)
    for shift, ref in ((1, to1_ref), (2, to2_ref), (3, to3_ref)):
        ref[...] = total[:, lax.rem(rep + shift, REPS)].reshape(block).astype(BF16)


def matmul(place, own, other, weights, lanes):
    steps = 4
    chips = CHIPS // steps
    share = weights.shape[0] // (CHIPS * CORES * REPS)
    depth = weights.shape[1]
    split = weights.reshape(CHIPS, CORES, REPS * share, depth)
    sent = jax.ShapeDtypeStruct((CHIPS * share, lanes), BF16)
    block = pl.BlockSpec((chips * share, lanes), lambda i, place: (i, 0))
    return pl.pallas_call(
        matmul_kernel,
        grid_spec=pltpu.PrefetchScalarGridSpec(
            num_scalar_prefetch=1,
            grid=(steps,),
            in_specs=[
                pl.BlockSpec(memory_space=pl.ANY),
                pl.BlockSpec(memory_space=pl.ANY),
                pl.BlockSpec(
                    (chips, 1, REPS * share, depth), lambda i, place: (i, place[0], 0, 0)
                ),
            ],
            out_specs=[block] * 4,
            scratch_shapes=[
                pltpu.VMEM((CHIPS, CORES, own.shape[1], lanes), BF16),
                pltpu.VMEM((chips, REPS, share, lanes), F32),
                pltpu.SemaphoreType.DMA((2,)),
            ],
        ),
        out_shape=[jax.ShapeDtypeStruct(sent.shape, F32), sent, sent, sent],
        compiler_params=pltpu.CompilerParams(vmem_limit_bytes=40 * 1024 * 1024),
    )(place, own, other, split)


def update_kernel(starts, tiles, ladder_ref, rest_ref, occupied_ref, virtual_ref, out_ref):
    virtual_sum = virtual_ref[...]
    for h, start in enumerate(starts):
        stop = starts[h + 1] if h + 1 < CHIPS else tiles
        lanes = slice(start * TILE, stop * TILE)
        ladder = ladder_ref[h, :, : (stop - start) * TILE].astype(F32)
        denominator = occupied_ref[:, lanes] - virtual_sum
        out_ref[:, lanes] = ((ladder + rest_ref[:, lanes].astype(F32)) / denominator).astype(BF16)


def update(ladder, rest, occupied_sum, virtual_sum, starts):
    return pl.pallas_call(
        functools.partial(update_kernel, starts, rest.shape[1] // TILE),
        out_shape=jax.ShapeDtypeStruct(rest.shape, BF16),
        compiler_params=pltpu.CompilerParams(vmem_limit_bytes=16 * 1024 * 1024),
    )(ladder, rest, occupied_sum, virtual_sum)


def energy_sums(occupied, virtual, slab_start, pair_count, share):
    occupied_sum = (occupied[:, None] + occupied[None, :]).reshape(-1)[:pair_count]
    place = (lax.axis_index("z") * Y + lax.axis_index("y")) * CORES + lax.axis_index("core")
    row_base = (place * REPS + lax.axis_index("rep")) * share
    count = virtual.shape[0]
    pair_index = slab_start[0] + row_base + jnp.arange(share, dtype=jnp.int32)
    ids = jnp.arange(count, dtype=jnp.int32)
    pick_first = (pair_index // count)[:, None] == ids[None, :]
    pick_second = (pair_index % count)[:, None] == ids[None, :]
    zero = F32(0.0)
    first = jnp.sum(jnp.where(pick_first, virtual[None, :], zero), axis=1)
    second = jnp.sum(jnp.where(pick_second, virtual[None, :], zero), axis=1)
    return occupied_sum[None, :], (first + second)[:, None]


def shifted(array, axis, size, shift):
    return lax.ppermute(array, axis, [(i, (i + shift) % size) for i in range(size)])


def on_device(amplitudes, integrals, rest_terms, occupied_energy, virtual_energy, slab_start):
    amp = amplitudes[:, 0, :].T
    weights = integrals[:, 0, :]
    share, pair_count = rest_terms.shape
    tiles = pair_count // TILE
    width = -(-tiles // CHIPS)
    lanes = width * TILE
    starts = tile_starts(tiles, width)
    occupied_sum, virtual_sum = energy_sums(
        occupied_energy, virtual_energy, slab_start, pair_count, share
    )
    place = jnp.stack([lax.axis_index("core"), lax.axis_index("rep")]).astype(jnp.int32)

    sent = repack(amp, starts, lanes)
    own = lax.all_to_all(sent, ("z", "y"), split_axis=0, concat_axis=0, tiled=True)
    other = shifted(own, "core", CORES, 1)
    keep, to1, to2, to3 = matmul(place, own, other, weights, lanes)
    got2 = shifted(to2, "rep", REPS, 2)
    got1 = shifted(to1, "rep", REPS, 1)
    got3 = shifted(to3, "rep", REPS, 3)
    total = keep + got1.astype(F32) + got2.astype(F32) + got3.astype(F32)
    blocks = total.astype(BF16).reshape(CHIPS, share, lanes)
    ladder = lax.all_to_all(blocks, ("z", "y"), split_axis=0, concat_axis=0, tiled=True)
    return update(ladder, rest_terms, occupied_sum, virtual_sum, starts)


def solution(mesh):
    axes = ("z", "y", "core", "rep")
    split = Mesh(mesh.devices.reshape(Z, Y, CORES, REPS), axes)
    grid = axes[:3]
    placed = (P(None, "rep", grid), P(None, "rep", None), P(axes, None), P(), P(), P())
    return jax.shard_map(
        on_device, mesh=split, in_specs=placed, out_specs=P(axes, None), check_vma=False
    )
```

```python
import functools

import jax
import jax.numpy as jnp
from jax import lax
from jax.experimental import pallas as pl
from jax.experimental.pallas import tpu as pltpu
from jax.sharding import Mesh, PartitionSpec as P

Z, Y, CORES, REPS = 8, 4, 2, 4
CHIPS = Z * Y
TILE, HALF = 128, 64
WHOLE = 5
CHUNKS = ((0, 4), (4, 2))
BF16, F32 = jnp.bfloat16, jnp.float32
ANY = pl.BlockSpec(memory_space=pl.ANY)
VMEM = pl.BlockSpec(memory_space=pltpu.VMEM)
SMEM = pl.BlockSpec(memory_space=pltpu.SMEM)
LIMIT = pltpu.CompilerParams(vmem_limit_bytes=24 * 1024 * 1024)


class Plan:
    def __init__(self, tiles):
        self.tiles = tiles
        halves, share = 2 * tiles, 2 * WHOLE + 1
        starts = [min(halves * h // CHIPS, halves - share) for h in range(CHIPS)]
        self.odd = [start % 2 for start in starts]
        self.first = [start // 2 + start % 2 for start in starts]
        self.split = [start // 2 if start % 2 else start // 2 + WHOLE for start in starts]

    def sources(self):
        whole, half = {}, {}
        for h in range(CHIPS):
            for place in range(WHOLE):
                whole.setdefault(self.first[h] + place, (h, place))
            half[self.split[h], self.odd[h]] = h
        return [
            (whole[tile], None) if tile in whole else (None, (half[tile, 0], half[tile, 1]))
            for tile in range(self.tiles)
        ]


def swap_halves(block):
    return jnp.concatenate([block[:, HALF:], block[:, :HALF]], axis=1)


def repack_kernel(plan, amp_ref, out_ref):
    depth = amp_ref.shape[0]
    third = depth // 3
    low = lax.broadcasted_iota(jnp.int32, (third, TILE), 1) < HALF
    for h in range(CHIPS):
        for place in range(WHOLE):
            start = (plan.first[h] + place) * TILE
            out_ref[h, place * depth : (place + 1) * depth] = amp_ref[:, start : start + TILE]
        block = amp_ref[:, plan.split[h] * TILE : (plan.split[h] + 1) * TILE].astype(F32)
        other = swap_halves(block)
        if plan.odd[h]:
            block, other = other, block
        packed = jnp.where(low, block[:third], other[third : 2 * third])
        out_ref[h, WHOLE * depth : WHOLE * depth + third] = packed.astype(BF16)
        out_ref[h, WHOLE * depth + third : WHOLE * depth + 2 * third] = block[2 * third :].astype(BF16)


def repack(plan, amp):
    depth = amp.shape[0]
    return pl.pallas_call(
        functools.partial(repack_kernel, plan),
        out_shape=jax.ShapeDtypeStruct((CHIPS, WHOLE * depth + 2 * depth // 3, TILE), BF16),
        in_specs=[VMEM],
        out_specs=VMEM,
        compiler_params=LIMIT,
    )(amp)


def hold_kernel(place_ref, weight_ref, _, out_ref, sem):
    core = place_ref[2]
    copies = [
        pltpu.make_async_copy(weight_ref.at[h, core], out_ref.at[h], sem.at[h]) for h in range(CHIPS)
    ]
    for copy in copies:
        copy.start()
    for copy in copies:
        copy.wait()


def hold(place, weights, own):
    chips, _, height, depth = weights.shape
    return pl.pallas_call(
        hold_kernel,
        out_shape=jax.ShapeDtypeStruct((chips, height, depth), BF16),
        in_specs=[SMEM, ANY, ANY],
        out_specs=VMEM,
        scratch_shapes=[pltpu.SemaphoreType.DMA((chips,))],
        compiler_params=pltpu.CompilerParams(vmem_limit_bytes=14 * 1024 * 1024),
    )(place, pltpu.with_memory_space_constraint(weights, pltpu.HBM), own)


def tile_of(ref, place, depth):
    if place < WHOLE:
        return ref[:, place * depth : (place + 1) * depth]
    third = depth // 3
    packed = ref[:, WHOLE * depth : WHOLE * depth + third].astype(F32)
    swapped = jnp.concatenate([packed[:, :, HALF:], packed[:, :, :HALF]], axis=2)
    last = ref[:, WHOLE * depth + third : WHOLE * depth + 2 * third]
    return jnp.concatenate([packed.astype(BF16), swapped.astype(BF16), last], axis=1)


def matmul_kernel(
    chunk, place_ref, own_ref, other_ref, weight_ref, keep_ref, to1_ref, to2_ref, to3_ref, rows, total
):
    core, rep = place_ref[2], place_ref[3]
    chips, share = total.shape[0], total.shape[2]
    height = chips * weight_ref.shape[1]
    depth = weight_ref.shape[2]
    block = chips * share
    first = core == 0
    for i in range(chunk[1]):
        own = tile_of(own_ref, chunk[0] + i, rows.shape[2])
        other = tile_of(other_ref, chunk[0] + i, rows.shape[2])
        lanes = slice(i * TILE, (i + 1) * TILE)
        rows[:, 0, :, lanes] = jnp.where(first, own, other)
        rows[:, 1, :, lanes] = jnp.where(first, other, own)
    step = total.shape[3]
    for i in range(CHIPS // chips):
        left = weight_ref[i * chips : (i + 1) * chips].reshape(height, depth)
        here = slice(i * block, (i + 1) * block)
        for start in range(0, rows.shape[3], step):
            lanes = slice(start, start + step)
            right = rows[:, :, :, lanes].reshape(depth, step)
            term = jnp.dot(left, right, preferred_element_type=F32)
            total[...] = term.reshape(total.shape)
            keep_ref[here, lanes] = total[:, pl.ds(rep, 1)].reshape(block, step)
            for shift, ref in ((1, to1_ref), (2, to2_ref), (3, to3_ref)):
                sent = total[:, pl.ds(lax.rem(rep + shift, REPS), 1)].reshape(block, step)
                ref[here, lanes] = sent.astype(BF16)


def matmul(chunk, place, own, other, weights):
    chips, height, depth = weights.shape
    share = height // REPS
    lanes = chunk[1] * TILE
    shape = (CHIPS * share, lanes)
    return pl.pallas_call(
        functools.partial(matmul_kernel, chunk),
        out_shape=[jax.ShapeDtypeStruct(shape, F32)] + [jax.ShapeDtypeStruct(shape, BF16)] * 3,
        in_specs=[SMEM] + [VMEM] * 3,
        out_specs=[VMEM] * 4,
        scratch_shapes=[
            pltpu.VMEM((CHIPS, CORES, depth // (CHIPS * CORES), lanes), BF16),
            pltpu.VMEM((8, REPS, share, 2 * TILE), F32),
        ],
        compiler_params=LIMIT,
        cost_estimate=pl.CostEstimate(
            flops=2 * chips * height * depth * lanes,
            bytes_accessed=2 * chips * height * depth,
            transcendentals=0,
        ),
    )(place, own, other, weights)


def update_kernel(plan, ladder_ref, rest_ref, occupied_ref, virtual_ref, out_ref):
    virtual_sum = virtual_ref[...]
    low = lax.broadcasted_iota(jnp.int32, (ladder_ref.shape[1], TILE), 1) < HALF
    half = slice(WHOLE * TILE, (WHOLE + 1) * TILE)
    for tile, (whole, halves) in enumerate(plan.sources()):
        lanes = slice(tile * TILE, (tile + 1) * TILE)
        if whole is not None:
            h, place = whole
            ladder = ladder_ref[h, :, place * TILE : (place + 1) * TILE].astype(F32)
        else:
            left, right = (ladder_ref[h, :, half].astype(F32) for h in halves)
            ladder = jnp.where(low, left, swap_halves(right))
        denominator = occupied_ref[:, lanes] - virtual_sum
        total = ladder + rest_ref[:, lanes].astype(F32)
        out_ref[:, lanes] = (total / denominator).astype(BF16)


def update(plan, ladder, rest, occupied_sum, virtual_sum):
    return pl.pallas_call(
        functools.partial(update_kernel, plan),
        out_shape=jax.ShapeDtypeStruct(rest.shape, BF16),
        compiler_params=LIMIT,
    )(ladder, rest, occupied_sum, virtual_sum)


def energy_sums(occupied, virtual, slab_start, pair_count, share):
    occupied_sum = (occupied[:, None] + occupied[None, :]).reshape(-1)[:pair_count]
    place = (lax.axis_index("z") * Y + lax.axis_index("y")) * CORES + lax.axis_index("core")
    row_base = (place * REPS + lax.axis_index("rep")) * share
    count = virtual.shape[0]
    pair_index = slab_start[0] + row_base + jnp.arange(share, dtype=jnp.int32)
    ids = jnp.arange(count, dtype=jnp.int32)
    pick_first = (pair_index // count)[:, None] == ids[None, :]
    pick_second = (pair_index % count)[:, None] == ids[None, :]
    zero = F32(0.0)
    first = jnp.sum(jnp.where(pick_first, virtual[None, :], zero), axis=1)
    second = jnp.sum(jnp.where(pick_second, virtual[None, :], zero), axis=1)
    return occupied_sum[None, :], (first + second)[:, None]


def shifted(array, axis, size, shift):
    return lax.ppermute(array, axis, [(i, (i + shift) % size) for i in range(size)])


def after(array, others):
    return lax.optimization_barrier((array, *others))[0]


def over_rep(chunk, place, own, other, weights):
    keep, to1, to2, to3 = matmul(chunk, place, own, other, weights)
    got2 = shifted(to2, "rep", REPS, 2)
    got1 = shifted(to1, "rep", REPS, 1)
    got3 = shifted(to3, "rep", REPS, 3)
    total = keep + got1.astype(F32) + got2.astype(F32) + got3.astype(F32)
    return total.astype(BF16)


def on_device(amplitudes, integrals, rest_terms, occupied_energy, virtual_energy, slab_start):
    amp = amplitudes[:, 0, :].T
    share, pair_count = rest_terms.shape
    plan = Plan(pair_count // TILE)
    occupied_sum, virtual_sum = energy_sums(
        occupied_energy, virtual_energy, slab_start, pair_count, share
    )
    place = jnp.stack([lax.axis_index(a) for a in ("z", "y", "core", "rep")]).astype(jnp.int32)
    split = integrals.reshape(CHIPS, CORES, REPS * share, integrals.shape[2])

    own = lax.all_to_all(repack(plan, amp), ("z", "y"), split_axis=0, concat_axis=0, tiled=True)
    other = shifted(own, "core", CORES, 1)
    weights = hold(place, split, own)
    totals = [over_rep(chunk, place, own, other, weights) for chunk in CHUNKS]
    total = jnp.concatenate(totals, axis=1)
    ladder = lax.all_to_all(
        total.reshape(CHIPS, share, -1), ("z", "y"), split_axis=0, concat_axis=0, tiled=True
    )
    return update(plan, ladder, rest_terms, occupied_sum, virtual_sum)


def solution(mesh):
    axes = ("z", "y", "core", "rep")
    split = Mesh(mesh.devices.reshape(Z, Y, CORES, REPS), axes)
    grid = axes[:3]
    placed = (P(None, "rep", grid), P(None, "rep", None), P(axes, None), P(), P(), P())
    return jax.shard_map(
        on_device, mesh=split, in_specs=placed, out_specs=P(axes, None), check_vma=False
    )
```

```python
import functools

import jax
import jax.numpy as jnp
from jax import lax
from jax.experimental import pallas as pl
from jax.experimental.pallas import tpu as pltpu
from jax.sharding import Mesh, PartitionSpec as P

Z, Y, CORES, REPS = 8, 4, 2, 4
CHIPS = Z * Y
TILE, HALF = 128, 64
WHOLE = 5
TILES = WHOLE + 1
STEP = 2 * TILE
BF16, F32 = jnp.bfloat16, jnp.float32
ANY = pl.BlockSpec(memory_space=pl.ANY)
VMEM = pl.BlockSpec(memory_space=pltpu.VMEM)
SMEM = pl.BlockSpec(memory_space=pltpu.SMEM)
LIMIT = pltpu.CompilerParams(vmem_limit_bytes=24 * 1024 * 1024)


class Plan:
    def __init__(self, tiles):
        self.tiles = tiles
        halves, share = 2 * tiles, 2 * WHOLE + 1
        starts = [min(halves * h // CHIPS, halves - share) for h in range(CHIPS)]
        self.odd = [start % 2 for start in starts]
        self.first = [start // 2 + start % 2 for start in starts]
        self.split = [start // 2 if start % 2 else start // 2 + WHOLE for start in starts]

    def sources(self):
        whole, half = {}, {}
        for h in range(CHIPS):
            for place in range(WHOLE):
                whole.setdefault(self.first[h] + place, (h, place))
            half[self.split[h], self.odd[h]] = h
        return [
            (whole[tile], None) if tile in whole else (None, (half[tile, 0], half[tile, 1]))
            for tile in range(self.tiles)
        ]


def swap_halves(block):
    return jnp.concatenate([block[:, HALF:], block[:, :HALF]], axis=1)


def repack_kernel(plan, amp_ref, out_ref):
    depth = amp_ref.shape[0]
    third = depth // 3
    low = lax.broadcasted_iota(jnp.int32, (third, TILE), 1) < HALF
    for h in range(CHIPS):
        for place in range(WHOLE):
            start = (plan.first[h] + place) * TILE
            out_ref[h, place * depth : (place + 1) * depth] = amp_ref[:, start : start + TILE]
        block = amp_ref[:, plan.split[h] * TILE : (plan.split[h] + 1) * TILE].astype(F32)
        other = swap_halves(block)
        if plan.odd[h]:
            block, other = other, block
        packed = jnp.where(low, block[:third], other[third : 2 * third])
        out_ref[h, WHOLE * depth : WHOLE * depth + third] = packed.astype(BF16)
        out_ref[h, WHOLE * depth + third : WHOLE * depth + 2 * third] = block[2 * third :].astype(BF16)


def repack(plan, amp):
    depth = amp.shape[0]
    return pl.pallas_call(
        functools.partial(repack_kernel, plan),
        out_shape=jax.ShapeDtypeStruct((CHIPS, WHOLE * depth + 2 * depth // 3, TILE), BF16),
        in_specs=[VMEM],
        out_specs=VMEM,
        compiler_params=LIMIT,
    )(amp)


def hold_kernel(place_ref, weight_ref, _, out_ref, sem):
    core, rep = place_ref[2], place_ref[3]
    copies = [
        pltpu.make_async_copy(
            weight_ref.at[:, core, lax.rem(rep + k, REPS)], out_ref.at[k], sem.at[k]
        )
        for k in range(REPS)
    ]
    for copy in copies:
        copy.start()
    for copy in copies:
        copy.wait()


def hold(place, weights, own):
    chips, _, _, share, depth = weights.shape
    return pl.pallas_call(
        hold_kernel,
        out_shape=jax.ShapeDtypeStruct((REPS, chips, share, depth), BF16),
        in_specs=[SMEM, ANY, ANY],
        out_specs=VMEM,
        scratch_shapes=[pltpu.SemaphoreType.DMA((REPS,))],
        compiler_params=LIMIT,
    )(place, pltpu.with_memory_space_constraint(weights, pltpu.HBM), own)


def tile_of(ref, place, depth):
    if place < WHOLE:
        return ref[:, place * depth : (place + 1) * depth]
    third = depth // 3
    packed = ref[:, WHOLE * depth : WHOLE * depth + third].astype(F32)
    swapped = jnp.concatenate([packed[:, :, HALF:], packed[:, :, :HALF]], axis=2)
    last = ref[:, WHOLE * depth + third : WHOLE * depth + 2 * third]
    return jnp.concatenate([packed.astype(BF16), swapped.astype(BF16), last], axis=1)


def product(k, rows_ref, weight_ref, out_ref):
    _, chips, share, depth = weight_ref.shape
    left = weight_ref[k].reshape(chips * share, depth)
    for start in range(0, TILES * TILE, STEP):
        lanes = slice(start, start + STEP)
        right = rows_ref[:, :, :, lanes].reshape(depth, STEP)
        out_ref[:, lanes] = jnp.dot(left, right, preferred_element_type=F32).astype(out_ref.dtype)


def join_kernel(k, place_ref, own_ref, other_ref, weight_ref, out_ref, rows_ref):
    first = place_ref[2] == 0
    for i in range(TILES):
        own = tile_of(own_ref, i, rows_ref.shape[2])
        other = tile_of(other_ref, i, rows_ref.shape[2])
        lanes = slice(i * TILE, (i + 1) * TILE)
        rows_ref[:, 0, :, lanes] = jnp.where(first, own, other)
        rows_ref[:, 1, :, lanes] = jnp.where(first, other, own)
    product(k, rows_ref, weight_ref, out_ref)


def cost(weights):
    _, chips, share, depth = weights.shape
    return pl.CostEstimate(
        flops=2 * chips * share * depth * TILES * TILE,
        bytes_accessed=2 * chips * share * depth,
        transcendentals=0,
    )


def join(k, place, own, other, weights):
    _, chips, share, depth = weights.shape
    rows = (chips, CORES, depth // (chips * CORES), TILES * TILE)
    return pl.pallas_call(
        functools.partial(join_kernel, k),
        out_shape=[
            jax.ShapeDtypeStruct((chips * share, TILES * TILE), BF16),
            jax.ShapeDtypeStruct(rows, BF16),
        ],
        in_specs=[SMEM] + [VMEM] * 3,
        out_specs=[VMEM] * 2,
        compiler_params=LIMIT,
        cost_estimate=cost(weights),
    )(place, own, other, weights)


def matmul(k, rows, weights):
    _, chips, share, _ = weights.shape
    return pl.pallas_call(
        functools.partial(product, k),
        out_shape=jax.ShapeDtypeStruct((chips * share, TILES * TILE), BF16 if k else F32),
        in_specs=[VMEM] * 2,
        out_specs=VMEM,
        compiler_params=LIMIT,
        cost_estimate=cost(weights),
    )(rows, weights)


def add_kernel(total_ref, got_ref, out_ref):
    out_ref[...] = (total_ref[...] + got_ref[...].astype(F32)).astype(out_ref.dtype)


def add(total, got, dtype):
    return pl.pallas_call(
        add_kernel,
        out_shape=jax.ShapeDtypeStruct(total.shape, dtype),
        in_specs=[VMEM] * 2,
        out_specs=VMEM,
        compiler_params=LIMIT,
        cost_estimate=pl.CostEstimate(flops=total.size, bytes_accessed=10 * total.size, transcendentals=0),
    )(total, got)


def update_kernel(plan, ladder_ref, rest_ref, occupied_ref, virtual_ref, out_ref):
    virtual_sum = virtual_ref[...]
    low = lax.broadcasted_iota(jnp.int32, (ladder_ref.shape[1], TILE), 1) < HALF
    half = slice(WHOLE * TILE, (WHOLE + 1) * TILE)
    for tile, (whole, halves) in enumerate(plan.sources()):
        lanes = slice(tile * TILE, (tile + 1) * TILE)
        if whole is not None:
            h, place = whole
            ladder = ladder_ref[h, :, place * TILE : (place + 1) * TILE].astype(F32)
        else:
            left, right = (ladder_ref[h, :, half].astype(F32) for h in halves)
            ladder = jnp.where(low, left, swap_halves(right))
        denominator = occupied_ref[:, lanes] - virtual_sum
        total = ladder + rest_ref[:, lanes].astype(F32)
        out_ref[:, lanes] = (total / denominator).astype(BF16)


def update(plan, ladder, rest, occupied_sum, virtual_sum):
    return pl.pallas_call(
        functools.partial(update_kernel, plan),
        out_shape=jax.ShapeDtypeStruct(rest.shape, BF16),
        compiler_params=LIMIT,
    )(ladder, rest, occupied_sum, virtual_sum)


def energy_sums(occupied, virtual, slab_start, pair_count, share):
    occupied_sum = (occupied[:, None] + occupied[None, :]).reshape(-1)[:pair_count]
    place = (lax.axis_index("z") * Y + lax.axis_index("y")) * CORES + lax.axis_index("core")
    row_base = (place * REPS + lax.axis_index("rep")) * share
    count = virtual.shape[0]
    pair_index = slab_start[0] + row_base + jnp.arange(share, dtype=jnp.int32)
    ids = jnp.arange(count, dtype=jnp.int32)
    pick_first = (pair_index // count)[:, None] == ids[None, :]
    pick_second = (pair_index % count)[:, None] == ids[None, :]
    zero = F32(0.0)
    first = jnp.sum(jnp.where(pick_first, virtual[None, :], zero), axis=1)
    second = jnp.sum(jnp.where(pick_second, virtual[None, :], zero), axis=1)
    return occupied_sum[None, :], (first + second)[:, None]


def shifted(array, axis, size, shift):
    return lax.ppermute(array, axis, [(i, (i + shift) % size) for i in range(size)])


def after(array, others):
    return lax.optimization_barrier((array, *others))[0]


def over_rep(place, own, other, weights):
    to2, rows = join(2, place, own, other, weights)
    got2 = shifted(to2, "rep", REPS, 2)
    got1 = shifted(matmul(1, rows, weights), "rep", REPS, 1)
    got3 = shifted(matmul(3, rows, weights), "rep", REPS, 3)
    total = add(matmul(0, rows, weights), got2, F32)
    total = add(total, got1, F32)
    return add(total, got3, BF16)


def on_device(amplitudes, integrals, rest_terms, occupied_energy, virtual_energy, slab_start):
    amp = amplitudes[:, 0, :].T
    share, pair_count = rest_terms.shape
    plan = Plan(pair_count // TILE)
    occupied_sum, virtual_sum = energy_sums(
        occupied_energy, virtual_energy, slab_start, pair_count, share
    )
    place = jnp.stack([lax.axis_index(a) for a in ("z", "y", "core", "rep")]).astype(jnp.int32)
    split = integrals.reshape(CHIPS, CORES, REPS, share, integrals.shape[2])

    own = lax.all_to_all(repack(plan, amp), ("z", "y"), split_axis=0, concat_axis=0, tiled=True)
    other = shifted(own, "core", CORES, 1)
    weights = hold(place, split, own)
    total = over_rep(place, own, other, weights)
    ladder = lax.all_to_all(
        total.reshape(CHIPS, share, -1), ("z", "y"), split_axis=0, concat_axis=0, tiled=True
    )
    return update(plan, ladder, rest_terms, occupied_sum, virtual_sum)


def solution(mesh):
    axes = ("z", "y", "core", "rep")
    split = Mesh(mesh.devices.reshape(Z, Y, CORES, REPS), axes)
    grid = axes[:3]
    placed = (P(None, "rep", grid), P(None, "rep", None), P(axes, None), P(), P(), P())
    return jax.shard_map(
        on_device, mesh=split, in_specs=placed, out_specs=P(axes, None), check_vma=False
    )
```

```python
import functools

import jax
import jax.numpy as jnp
from jax import lax
from jax.experimental import pallas as pl
from jax.experimental.pallas import tpu as pltpu
from jax.sharding import Mesh, PartitionSpec as P

Z, Y, CORES, REPS = 8, 4, 2, 4
CHIPS = Z * Y
TILE, HALF = 128, 64
WHOLE = 5
TILES = WHOLE + 1
STEP = 2 * TILE
ORDER = (2, 1, 3)
PIECES = (1, 1, 1, 1)
BF16, F32 = jnp.bfloat16, jnp.float32
ANY = pl.BlockSpec(memory_space=pl.ANY)
VMEM = pl.BlockSpec(memory_space=pltpu.VMEM)
SMEM = pl.BlockSpec(memory_space=pltpu.SMEM)
LIMIT = pltpu.CompilerParams(vmem_limit_bytes=24 * 1024 * 1024)


class Plan:
    def __init__(self, tiles):
        self.tiles = tiles
        halves, share = 2 * tiles, 2 * WHOLE + 1
        starts = [min(halves * h // CHIPS, halves - share) for h in range(CHIPS)]
        self.odd = [start % 2 for start in starts]
        self.first = [start // 2 + start % 2 for start in starts]
        self.split = [start // 2 if start % 2 else start // 2 + WHOLE for start in starts]

    def sources(self):
        whole, half = {}, {}
        for h in range(CHIPS):
            for place in range(WHOLE):
                whole.setdefault(self.first[h] + place, (h, place))
            half[self.split[h], self.odd[h]] = h
        return [
            (whole[tile], None) if tile in whole else (None, (half[tile, 0], half[tile, 1]))
            for tile in range(self.tiles)
        ]


def swap_halves(block):
    return jnp.concatenate([block[:, HALF:], block[:, :HALF]], axis=1)


def repack_kernel(plan, amp_ref, out_ref):
    depth = amp_ref.shape[0]
    third = depth // 3
    low = lax.broadcasted_iota(jnp.int32, (third, TILE), 1) < HALF
    for h in range(CHIPS):
        for place in range(WHOLE):
            start = (plan.first[h] + place) * TILE
            out_ref[h, place * depth : (place + 1) * depth] = amp_ref[:, start : start + TILE]
        block = amp_ref[:, plan.split[h] * TILE : (plan.split[h] + 1) * TILE].astype(F32)
        other = swap_halves(block)
        if plan.odd[h]:
            block, other = other, block
        packed = jnp.where(low, block[:third], other[third : 2 * third])
        out_ref[h, WHOLE * depth : WHOLE * depth + third] = packed.astype(BF16)
        out_ref[h, WHOLE * depth + third : WHOLE * depth + 2 * third] = block[2 * third :].astype(BF16)


def repack(plan, amp):
    depth = amp.shape[0]
    return pl.pallas_call(
        functools.partial(repack_kernel, plan),
        out_shape=jax.ShapeDtypeStruct((CHIPS, WHOLE * depth + 2 * depth // 3, TILE), BF16),
        in_specs=[VMEM],
        out_specs=VMEM,
        compiler_params=LIMIT,
    )(amp)


def hold_kernel(place_ref, weight_ref, _, out_ref, sem):
    core, rep = place_ref[2], place_ref[3]
    copies = [
        pltpu.make_async_copy(
            weight_ref.at[:, core, lax.rem(rep + k, REPS)], out_ref.at[k], sem.at[k]
        )
        for k in range(REPS)
    ]
    for copy in copies:
        copy.start()
    for copy in copies:
        copy.wait()


def hold(place, weights, own):
    chips, _, _, share, depth = weights.shape
    return pl.pallas_call(
        hold_kernel,
        out_shape=jax.ShapeDtypeStruct((REPS, chips, share, depth), BF16),
        in_specs=[SMEM, ANY, ANY],
        out_specs=VMEM,
        scratch_shapes=[pltpu.SemaphoreType.DMA((REPS,))],
        compiler_params=LIMIT,
    )(place, pltpu.with_memory_space_constraint(weights, pltpu.HBM), own)


def tile_of(ref, place, depth):
    if place < WHOLE:
        return ref[:, place * depth : (place + 1) * depth]
    third = depth // 3
    packed = ref[:, WHOLE * depth : WHOLE * depth + third].astype(F32)
    swapped = jnp.concatenate([packed[:, :, HALF:], packed[:, :, :HALF]], axis=2)
    last = ref[:, WHOLE * depth + third : WHOLE * depth + 2 * third]
    return jnp.concatenate([packed.astype(BF16), swapped.astype(BF16), last], axis=1)


def product(k, rows_ref, weight_ref, outs):
    _, chips, share, depth = weight_ref.shape
    height = chips * share
    left = weight_ref[k].reshape(height, depth)
    parts = []
    for start in range(0, TILES * TILE, STEP):
        right = rows_ref[:, :, :, start : start + STEP].reshape(depth, STEP)
        term = jnp.dot(left, right, preferred_element_type=F32)
        parts += [term[:, :TILE], term[:, TILE:]]
    low = lax.broadcasted_iota(jnp.int32, (height // 2, TILE), 1) < HALF
    last = parts.pop()
    parts.append(jnp.where(low, last[: height // 2], swap_halves(last[height // 2 :])))
    at, end = 0, outs[0].shape[0]
    place = 0
    for part in parts:
        part = part.astype(outs[0].dtype)
        done = 0
        while done < part.shape[0]:
            size = min(part.shape[0] - done, end - at)
            outs[place][at : at + size] = part[done : done + size]
            at, done = at + size, done + size
            if at == end:
                place, at = place + 1, 0


def join_kernel(k, place_ref, own_ref, other_ref, weight_ref, rows_ref, *outs):
    first = place_ref[2] == 0
    for i in range(TILES):
        own = tile_of(own_ref, i, rows_ref.shape[2])
        other = tile_of(other_ref, i, rows_ref.shape[2])
        lanes = slice(i * TILE, (i + 1) * TILE)
        rows_ref[:, 0, :, lanes] = jnp.where(first, own, other)
        rows_ref[:, 1, :, lanes] = jnp.where(first, other, own)
    product(k, rows_ref, weight_ref, outs)


def cost(weights):
    _, chips, share, depth = weights.shape
    return pl.CostEstimate(
        flops=2 * chips * share * depth * TILES * TILE,
        bytes_accessed=2 * chips * share * depth,
        transcendentals=0,
    )


def packed(weights, pieces, dtype):
    height = weights.shape[1] * weights.shape[2]
    return [jax.ShapeDtypeStruct(((2 * WHOLE + 1) * height // 2 // pieces, TILE), dtype)] * pieces


def join(k, place, own, other, weights):
    _, chips, _, depth = weights.shape
    rows = (chips, CORES, depth // (chips * CORES), TILES * TILE)
    rows, *outs = pl.pallas_call(
        functools.partial(join_kernel, k),
        out_shape=[jax.ShapeDtypeStruct(rows, BF16)] + packed(weights, PIECES[k], BF16),
        in_specs=[SMEM] + [VMEM] * 3,
        out_specs=[VMEM] * (1 + PIECES[k]),
        compiler_params=LIMIT,
        cost_estimate=cost(weights),
    )(place, own, other, weights)
    return outs, rows


def matmul_kernel(k, rows_ref, weight_ref, *outs):
    product(k, rows_ref, weight_ref, outs)


def matmul(k, rows, weights):
    return pl.pallas_call(
        functools.partial(matmul_kernel, k),
        out_shape=packed(weights, PIECES[k], BF16 if k else F32),
        in_specs=[VMEM] * 2,
        out_specs=[VMEM] * PIECES[k],
        compiler_params=LIMIT,
        cost_estimate=cost(weights),
    )(rows, weights)


def add_kernel(total_ref, *refs):
    gots, out_ref = refs[:-1], refs[-1]
    size = gots[0].shape[0]
    for i, got in enumerate(gots):
        here = slice(i * size, (i + 1) * size)
        out_ref[here] = total_ref[here] + got[...].astype(F32)


def add_last_kernel(total_ref, *refs):
    gots, out_ref = refs[:-1], refs[-1]
    size, height = gots[0].shape[0], out_ref.shape[0]
    whole = jnp.concatenate([got[...].astype(F32) for got in gots], axis=0) + total_ref[...]
    for place in range(WHOLE):
        part = whole[place * height : (place + 1) * height]
        out_ref[:, place * TILE : (place + 1) * TILE] = part.astype(BF16)
    part = whole[WHOLE * height :]
    part = jnp.concatenate([part, swap_halves(part)], axis=0)
    out_ref[:, WHOLE * TILE :] = part.astype(BF16)


def add(total, gots, last=False):
    height = 2 * total.shape[0] // (2 * WHOLE + 1)
    shape = jax.ShapeDtypeStruct((height, TILES * TILE), BF16)
    return pl.pallas_call(
        add_last_kernel if last else add_kernel,
        out_shape=shape if last else jax.ShapeDtypeStruct(total.shape, F32),
        in_specs=[VMEM] * (1 + len(gots)),
        out_specs=VMEM,
        compiler_params=LIMIT,
        cost_estimate=pl.CostEstimate(
            flops=total.size, bytes_accessed=10 * total.size, transcendentals=0
        ),
    )(total, *gots)


def update_kernel(plan, ladder_ref, rest_ref, occupied_ref, virtual_ref, out_ref):
    virtual_sum = virtual_ref[...]
    low = lax.broadcasted_iota(jnp.int32, (ladder_ref.shape[1], TILE), 1) < HALF
    half = slice(WHOLE * TILE, (WHOLE + 1) * TILE)
    for tile, (whole, halves) in enumerate(plan.sources()):
        lanes = slice(tile * TILE, (tile + 1) * TILE)
        if whole is not None:
            h, place = whole
            ladder = ladder_ref[h, :, place * TILE : (place + 1) * TILE].astype(F32)
        else:
            left, right = (ladder_ref[h, :, half].astype(F32) for h in halves)
            ladder = jnp.where(low, left, swap_halves(right))
        denominator = occupied_ref[:, lanes] - virtual_sum
        total = ladder + rest_ref[:, lanes].astype(F32)
        out_ref[:, lanes] = (total / denominator).astype(BF16)


def update(plan, ladder, rest, occupied_sum, virtual_sum):
    return pl.pallas_call(
        functools.partial(update_kernel, plan),
        out_shape=jax.ShapeDtypeStruct(rest.shape, BF16),
        compiler_params=LIMIT,
    )(ladder, rest, occupied_sum, virtual_sum)


def energy_sums(occupied, virtual, slab_start, pair_count, share):
    occupied_sum = (occupied[:, None] + occupied[None, :]).reshape(-1)[:pair_count]
    place = (lax.axis_index("z") * Y + lax.axis_index("y")) * CORES + lax.axis_index("core")
    row_base = (place * REPS + lax.axis_index("rep")) * share
    count = virtual.shape[0]
    pair_index = slab_start[0] + row_base + jnp.arange(share, dtype=jnp.int32)
    ids = jnp.arange(count, dtype=jnp.int32)
    pick_first = (pair_index // count)[:, None] == ids[None, :]
    pick_second = (pair_index % count)[:, None] == ids[None, :]
    zero = F32(0.0)
    first = jnp.sum(jnp.where(pick_first, virtual[None, :], zero), axis=1)
    second = jnp.sum(jnp.where(pick_second, virtual[None, :], zero), axis=1)
    return occupied_sum[None, :], (first + second)[:, None]


def shifted(array, axis, size, shift):
    return lax.ppermute(array, axis, [(i, (i + shift) % size) for i in range(size)])


def after(array, others):
    return lax.optimization_barrier((array, *others))[0]


def over_rep(place, own, other, weights):
    sent, rows = join(ORDER[0], place, own, other, weights)
    got = []
    for k in ORDER:
        blocks = sent if k == ORDER[0] else matmul(k, rows, weights)
        got.append([shifted(block, "rep", REPS, k) for block in blocks])
    total = matmul(0, rows, weights)[0]
    for blocks in got[:-1]:
        total = add(total, blocks)
    return add(total, got[-1], last=True)


def on_device(amplitudes, integrals, rest_terms, occupied_energy, virtual_energy, slab_start):
    amp = amplitudes[:, 0, :].T
    share, pair_count = rest_terms.shape
    plan = Plan(pair_count // TILE)
    occupied_sum, virtual_sum = energy_sums(
        occupied_energy, virtual_energy, slab_start, pair_count, share
    )
    place = jnp.stack([lax.axis_index(a) for a in ("z", "y", "core", "rep")]).astype(jnp.int32)
    split = integrals.reshape(CHIPS, CORES, REPS, share, integrals.shape[2])

    own = lax.all_to_all(repack(plan, amp), ("z", "y"), split_axis=0, concat_axis=0, tiled=True)
    other = shifted(own, "core", CORES, 1)
    weights = hold(place, split, own)
    total = over_rep(place, own, other, weights)
    ladder = lax.all_to_all(
        total.reshape(CHIPS, share, -1), ("z", "y"), split_axis=0, concat_axis=0, tiled=True
    )
    return update(plan, ladder, rest_terms, occupied_sum, virtual_sum)


def solution(mesh):
    axes = ("z", "y", "core", "rep")
    split = Mesh(mesh.devices.reshape(Z, Y, CORES, REPS), axes)
    grid = axes[:3]
    placed = (P(None, "rep", grid), P(None, "rep", None), P(axes, None), P(), P(), P())
    return jax.shard_map(
        on_device, mesh=split, in_specs=placed, out_specs=P(axes, None), check_vma=False
    )
```

```python
import functools

import jax
import jax.numpy as jnp
from jax import lax
from jax.experimental import pallas as pl
from jax.experimental.pallas import tpu as pltpu
from jax.sharding import Mesh, PartitionSpec as P

Z, Y, CORES, REPS = 8, 4, 2, 4
CHIPS = Z * Y
TILE, HALF = 128, 64
WHOLE = 5
TILES = WHOLE + 1
STEP = 2 * TILE
ORDER = (1, 2, 3)
PIECES = (1, 1, 1, 1)
BF16, F32 = jnp.bfloat16, jnp.float32
ANY = pl.BlockSpec(memory_space=pl.ANY)
VMEM = pl.BlockSpec(memory_space=pltpu.VMEM)
SMEM = pl.BlockSpec(memory_space=pltpu.SMEM)
LIMIT = pltpu.CompilerParams(vmem_limit_bytes=24 * 1024 * 1024)


class Plan:
    def __init__(self, tiles):
        self.tiles = tiles
        halves, share = 2 * tiles, 2 * WHOLE + 1
        starts = [min(halves * h // CHIPS, halves - share) for h in range(CHIPS)]
        self.odd = [start % 2 for start in starts]
        self.first = [start // 2 + start % 2 for start in starts]
        self.split = [start // 2 if start % 2 else start // 2 + WHOLE for start in starts]

    def sources(self):
        whole, half = {}, {}
        for h in range(CHIPS):
            for place in range(WHOLE):
                whole.setdefault(self.first[h] + place, (h, place))
            half[self.split[h], self.odd[h]] = h
        return [
            (whole[tile], None) if tile in whole else (None, (half[tile, 0], half[tile, 1]))
            for tile in range(self.tiles)
        ]


def swap_halves(block):
    return jnp.concatenate([block[:, HALF:], block[:, :HALF]], axis=1)


def repack_kernel(plan, amp_ref, out_ref):
    depth = amp_ref.shape[0]
    middle = depth // 2
    low = lax.broadcasted_iota(jnp.int32, (middle, TILE), 1) < HALF
    for h in range(CHIPS):
        for place in range(WHOLE):
            start = (plan.first[h] + place) * TILE
            out_ref[h, place * depth : (place + 1) * depth] = amp_ref[:, start : start + TILE]
        block = amp_ref[:, plan.split[h] * TILE : (plan.split[h] + 1) * TILE].astype(F32)
        other = swap_halves(block)
        if plan.odd[h]:
            block, other = other, block
        packed = jnp.where(low, block[:middle], other[middle:])
        out_ref[h, WHOLE * depth :] = packed.astype(BF16)


def repack(plan, amp):
    depth = amp.shape[0]
    return pl.pallas_call(
        functools.partial(repack_kernel, plan),
        out_shape=jax.ShapeDtypeStruct((CHIPS, WHOLE * depth + depth // 2, TILE), BF16),
        in_specs=[VMEM],
        out_specs=VMEM,
        compiler_params=LIMIT,
    )(amp)


def hold_kernel(place_ref, weight_ref, _, out_ref, sem):
    core, rep = place_ref[2], place_ref[3]
    copies = [
        pltpu.make_async_copy(
            weight_ref.at[:, core, lax.rem(rep + k, REPS)], out_ref.at[k], sem.at[k]
        )
        for k in range(REPS)
    ]
    for copy in copies:
        copy.start()
    for copy in copies:
        copy.wait()


def hold(place, weights, own):
    chips, _, _, share, depth = weights.shape
    return pl.pallas_call(
        hold_kernel,
        out_shape=jax.ShapeDtypeStruct((REPS, chips, share, depth), BF16),
        in_specs=[SMEM, ANY, ANY],
        out_specs=VMEM,
        scratch_shapes=[pltpu.SemaphoreType.DMA((REPS,))],
        compiler_params=LIMIT,
    )(place, pltpu.with_memory_space_constraint(weights, pltpu.HBM), own)


def tile_of(ref, place, depth):
    if place < WHOLE:
        return ref[:, place * depth : (place + 1) * depth]
    packed = ref[:, WHOLE * depth :].astype(F32)
    swapped = jnp.concatenate([packed[:, :, HALF:], packed[:, :, :HALF]], axis=2)
    return jnp.concatenate([packed, swapped], axis=1).astype(BF16)


def product(k, rows_ref, weight_ref, outs):
    _, chips, share, depth = weight_ref.shape
    height = chips * share
    left = weight_ref[k].reshape(height, depth)
    parts = []
    for start in range(0, TILES * TILE, STEP):
        right = rows_ref[:, :, :, start : start + STEP].reshape(depth, STEP)
        term = jnp.dot(left, right, preferred_element_type=F32)
        parts += [term[:, :TILE], term[:, TILE:]]
    low = lax.broadcasted_iota(jnp.int32, (height // 2, TILE), 1) < HALF
    last = parts.pop()
    parts.append(jnp.where(low, last[: height // 2], swap_halves(last[height // 2 :])))
    at, end = 0, outs[0].shape[0]
    place = 0
    for part in parts:
        part = part.astype(outs[0].dtype)
        done = 0
        while done < part.shape[0]:
            size = min(part.shape[0] - done, end - at)
            outs[place][at : at + size] = part[done : done + size]
            at, done = at + size, done + size
            if at == end:
                place, at = place + 1, 0


def join_kernel(k, place_ref, own_ref, other_ref, weight_ref, rows_ref, *outs):
    first = place_ref[2] == 0
    for i in range(TILES):
        own = tile_of(own_ref, i, rows_ref.shape[2])
        other = tile_of(other_ref, i, rows_ref.shape[2])
        lanes = slice(i * TILE, (i + 1) * TILE)
        rows_ref[:, 0, :, lanes] = jnp.where(first, own, other)
        rows_ref[:, 1, :, lanes] = jnp.where(first, other, own)
    product(k, rows_ref, weight_ref, outs)


def cost(weights):
    _, chips, share, depth = weights.shape
    return pl.CostEstimate(
        flops=2 * chips * share * depth * TILES * TILE,
        bytes_accessed=2 * chips * share * depth,
        transcendentals=0,
    )


def packed(weights, pieces, dtype):
    height = weights.shape[1] * weights.shape[2]
    return [jax.ShapeDtypeStruct(((2 * WHOLE + 1) * height // 2 // pieces, TILE), dtype)] * pieces


def join(k, place, own, other, weights):
    _, chips, _, depth = weights.shape
    rows = (chips, CORES, depth // (chips * CORES), TILES * TILE)
    rows, *outs = pl.pallas_call(
        functools.partial(join_kernel, k),
        out_shape=[jax.ShapeDtypeStruct(rows, BF16)] + packed(weights, PIECES[k], BF16),
        in_specs=[SMEM] + [VMEM] * 3,
        out_specs=[VMEM] * (1 + PIECES[k]),
        compiler_params=LIMIT,
        cost_estimate=cost(weights),
    )(place, own, other, weights)
    return outs, rows


def matmul_kernel(k, rows_ref, weight_ref, *outs):
    product(k, rows_ref, weight_ref, outs)


def matmul(k, rows, weights):
    return pl.pallas_call(
        functools.partial(matmul_kernel, k),
        out_shape=packed(weights, PIECES[k], BF16 if k else F32),
        in_specs=[VMEM] * 2,
        out_specs=[VMEM] * PIECES[k],
        compiler_params=LIMIT,
        cost_estimate=cost(weights),
    )(rows, weights)


def add_kernel(total_ref, *refs):
    gots, out_ref = refs[:-1], refs[-1]
    size = gots[0].shape[0]
    for i, got in enumerate(gots):
        here = slice(i * size, (i + 1) * size)
        out_ref[here] = total_ref[here] + got[...].astype(F32)


def add_last_kernel(total_ref, *refs):
    gots, out_ref = refs[:-1], refs[-1]
    size, height = gots[0].shape[0], out_ref.shape[0]
    whole = jnp.concatenate([got[...].astype(F32) for got in gots], axis=0) + total_ref[...]
    for place in range(WHOLE):
        part = whole[place * height : (place + 1) * height]
        out_ref[:, place * TILE : (place + 1) * TILE] = part.astype(BF16)
    part = whole[WHOLE * height :]
    part = jnp.concatenate([part, swap_halves(part)], axis=0)
    out_ref[:, WHOLE * TILE :] = part.astype(BF16)


def add(total, gots, last=False):
    height = 2 * total.shape[0] // (2 * WHOLE + 1)
    shape = jax.ShapeDtypeStruct((height, TILES * TILE), BF16)
    return pl.pallas_call(
        add_last_kernel if last else add_kernel,
        out_shape=shape if last else jax.ShapeDtypeStruct(total.shape, F32),
        in_specs=[VMEM] * (1 + len(gots)),
        out_specs=VMEM,
        compiler_params=LIMIT,
        cost_estimate=pl.CostEstimate(
            flops=total.size, bytes_accessed=10 * total.size, transcendentals=0
        ),
    )(total, *gots)


def update_kernel(plan, ladder_ref, rest_ref, occupied_ref, virtual_ref, out_ref):
    virtual_sum = virtual_ref[...]
    low = lax.broadcasted_iota(jnp.int32, (ladder_ref.shape[1], TILE), 1) < HALF
    half = slice(WHOLE * TILE, (WHOLE + 1) * TILE)
    for tile, (whole, halves) in enumerate(plan.sources()):
        lanes = slice(tile * TILE, (tile + 1) * TILE)
        if whole is not None:
            h, place = whole
            ladder = ladder_ref[h, :, place * TILE : (place + 1) * TILE].astype(F32)
        else:
            left, right = (ladder_ref[h, :, half].astype(F32) for h in halves)
            ladder = jnp.where(low, left, swap_halves(right))
        denominator = occupied_ref[:, lanes] - virtual_sum
        total = ladder + rest_ref[:, lanes].astype(F32)
        out_ref[:, lanes] = (total / denominator).astype(BF16)


def update(plan, ladder, rest, occupied_sum, virtual_sum):
    return pl.pallas_call(
        functools.partial(update_kernel, plan),
        out_shape=jax.ShapeDtypeStruct(rest.shape, BF16),
        compiler_params=LIMIT,
    )(ladder, rest, occupied_sum, virtual_sum)


def energy_sums(occupied, virtual, slab_start, pair_count, share):
    occupied_sum = (occupied[:, None] + occupied[None, :]).reshape(-1)[:pair_count]
    place = (lax.axis_index("z") * Y + lax.axis_index("y")) * CORES + lax.axis_index("core")
    row_base = (place * REPS + lax.axis_index("rep")) * share
    count = virtual.shape[0]
    pair_index = slab_start[0] + row_base + jnp.arange(share, dtype=jnp.int32)
    ids = jnp.arange(count, dtype=jnp.int32)
    pick_first = (pair_index // count)[:, None] == ids[None, :]
    pick_second = (pair_index % count)[:, None] == ids[None, :]
    zero = F32(0.0)
    first = jnp.sum(jnp.where(pick_first, virtual[None, :], zero), axis=1)
    second = jnp.sum(jnp.where(pick_second, virtual[None, :], zero), axis=1)
    return occupied_sum[None, :], (first + second)[:, None]


def shifted(array, axis, size, shift):
    return lax.ppermute(array, axis, [(i, (i + shift) % size) for i in range(size)])


def after(array, others):
    return lax.optimization_barrier((array, *others))[0]


def over_rep(place, own, other, weights):
    sent, rows = join(ORDER[0], place, own, other, weights)
    got = []
    for k in ORDER:
        blocks = sent if k == ORDER[0] else matmul(k, rows, weights)
        got.append([shifted(block, "rep", REPS, k) for block in blocks])
    total = matmul(0, rows, weights)[0]
    for blocks in got[:-1]:
        total = add(total, blocks)
    return add(total, got[-1], last=True)


def on_device(amplitudes, integrals, rest_terms, occupied_energy, virtual_energy, slab_start):
    amp = amplitudes[:, 0, :].T
    share, pair_count = rest_terms.shape
    plan = Plan(pair_count // TILE)
    occupied_sum, virtual_sum = energy_sums(
        occupied_energy, virtual_energy, slab_start, pair_count, share
    )
    place = jnp.stack([lax.axis_index(a) for a in ("z", "y", "core", "rep")]).astype(jnp.int32)
    split = integrals.reshape(CHIPS, CORES, REPS, share, integrals.shape[2])

    sent, place = lax.optimization_barrier((repack(plan, amp), place))
    own = lax.all_to_all(sent, ("z", "y"), split_axis=0, concat_axis=0, tiled=True)
    other = shifted(own, "core", CORES, 1)
    weights = hold(place, split, own)
    total = over_rep(place, own, other, weights)
    ladder = lax.all_to_all(
        total.reshape(CHIPS, share, -1), ("z", "y"), split_axis=0, concat_axis=0, tiled=True
    )
    return update(plan, ladder, rest_terms, occupied_sum, virtual_sum)


def solution(mesh):
    axes = ("z", "y", "core", "rep")
    split = Mesh(mesh.devices.reshape(Z, Y, CORES, REPS), axes)
    grid = axes[:3]
    placed = (P(None, "rep", grid), P(None, "rep", None), P(axes, None), P(), P(), P())
    return jax.shard_map(
        on_device, mesh=split, in_specs=placed, out_specs=P(axes, None), check_vma=False
    )
```

```python
import functools

import jax
import jax.numpy as jnp
from jax import lax
from jax.experimental import pallas as pl
from jax.experimental.pallas import tpu as pltpu
from jax.sharding import Mesh, PartitionSpec as P

Z, Y, CORES, REPS = 8, 4, 2, 4
CHIPS = Z * Y
TILE, HALF = 128, 64
WHOLE = 5
COPIES = 4
TILES = WHOLE + 1
STEP = 2 * TILE
ORDER = (1, 2, 3)
PIECES = (1, 1, 1, 1)
BF16, F32 = jnp.bfloat16, jnp.float32
ANY = pl.BlockSpec(memory_space=pl.ANY)
VMEM = pl.BlockSpec(memory_space=pltpu.VMEM)
SMEM = pl.BlockSpec(memory_space=pltpu.SMEM)
LIMIT = pltpu.CompilerParams(vmem_limit_bytes=24 * 1024 * 1024)


class Plan:
    def __init__(self, tiles):
        self.tiles = tiles
        halves, share = 2 * tiles, 2 * WHOLE + 1
        starts = [min(halves * h // CHIPS, halves - share) for h in range(CHIPS)]
        self.odd = [start % 2 for start in starts]
        self.first = [start // 2 + start % 2 for start in starts]
        self.split = [start // 2 if start % 2 else start // 2 + WHOLE for start in starts]

    def sources(self):
        whole, half = {}, {}
        for h in range(CHIPS):
            for place in range(WHOLE):
                whole.setdefault(self.first[h] + place, (h, place))
            half[self.split[h], self.odd[h]] = h
        return [
            (whole[tile], None) if tile in whole else (None, (half[tile, 0], half[tile, 1]))
            for tile in range(self.tiles)
        ]


def swap_halves(block):
    return jnp.concatenate([block[:, HALF:], block[:, :HALF]], axis=1)


def repack_kernel(plan, source_ref, out_ref, amp_ref, sem):
    depth = amp_ref.shape[0]
    width = plan.tiles // COPIES
    copies = []
    for i in range(COPIES):
        here = pl.ds(i * width * TILE, width * TILE)
        copies.append(pltpu.make_async_copy(source_ref.at[:, here], amp_ref.at[:, here], sem.at[i]))
    for copy in copies:
        copy.start()
    arrived = 0
    middle = depth // 2
    low = lax.broadcasted_iota(jnp.int32, (middle, TILE), 1) < HALF
    for h in range(CHIPS):
        while arrived * width <= max(plan.first[h] + WHOLE - 1, plan.split[h]):
            copies[arrived].wait()
            arrived += 1
        for place in range(WHOLE):
            start = (plan.first[h] + place) * TILE
            out_ref[h, place * depth : (place + 1) * depth] = amp_ref[:, start : start + TILE]
        block = amp_ref[:, plan.split[h] * TILE : (plan.split[h] + 1) * TILE].astype(F32)
        other = swap_halves(block)
        if plan.odd[h]:
            block, other = other, block
        packed = jnp.where(low, block[:middle], other[middle:])
        out_ref[h, WHOLE * depth :] = packed.astype(BF16)


def repack(plan, amp):
    depth = amp.shape[0]
    return pl.pallas_call(
        functools.partial(repack_kernel, plan),
        out_shape=jax.ShapeDtypeStruct((CHIPS, WHOLE * depth + depth // 2, TILE), BF16),
        in_specs=[ANY],
        out_specs=VMEM,
        scratch_shapes=[pltpu.VMEM(amp.shape, BF16), pltpu.SemaphoreType.DMA((COPIES,))],
        compiler_params=LIMIT,
    )(pltpu.with_memory_space_constraint(amp, pltpu.HBM))


def hold_kernel(place_ref, weight_ref, _, out_ref, sem):
    core, rep = place_ref[2], place_ref[3]
    copies = [
        pltpu.make_async_copy(
            weight_ref.at[:, core, lax.rem(rep + k, REPS)], out_ref.at[k], sem.at[k]
        )
        for k in range(REPS)
    ]
    for copy in copies:
        copy.start()
    for copy in copies:
        copy.wait()


def hold(place, weights, own):
    chips, _, _, share, depth = weights.shape
    return pl.pallas_call(
        hold_kernel,
        out_shape=jax.ShapeDtypeStruct((REPS, chips, share, depth), BF16),
        in_specs=[SMEM, ANY, ANY],
        out_specs=VMEM,
        scratch_shapes=[pltpu.SemaphoreType.DMA((REPS,))],
        compiler_params=LIMIT,
    )(place, pltpu.with_memory_space_constraint(weights, pltpu.HBM), own)


def tile_of(ref, place, depth):
    if place < WHOLE:
        return ref[:, place * depth : (place + 1) * depth]
    packed = ref[:, WHOLE * depth :].astype(F32)
    swapped = jnp.concatenate([packed[:, :, HALF:], packed[:, :, :HALF]], axis=2)
    return jnp.concatenate([packed, swapped], axis=1).astype(BF16)


def product(k, rows_ref, weight_ref, outs):
    _, chips, share, depth = weight_ref.shape
    height = chips * share
    left = weight_ref[k].reshape(height, depth)
    parts = []
    for start in range(0, TILES * TILE, STEP):
        right = rows_ref[:, :, :, start : start + STEP].reshape(depth, STEP)
        term = jnp.dot(left, right, preferred_element_type=F32)
        parts += [term[:, :TILE], term[:, TILE:]]
    low = lax.broadcasted_iota(jnp.int32, (height // 2, TILE), 1) < HALF
    last = parts.pop()
    parts.append(jnp.where(low, last[: height // 2], swap_halves(last[height // 2 :])))
    at, end = 0, outs[0].shape[0]
    place = 0
    for part in parts:
        part = part.astype(outs[0].dtype)
        done = 0
        while done < part.shape[0]:
            size = min(part.shape[0] - done, end - at)
            outs[place][at : at + size] = part[done : done + size]
            at, done = at + size, done + size
            if at == end:
                place, at = place + 1, 0


def join_kernel(k, place_ref, own_ref, other_ref, weight_ref, rows_ref, *outs):
    first = place_ref[2] == 0
    for i in range(TILES):
        own = tile_of(own_ref, i, rows_ref.shape[2])
        other = tile_of(other_ref, i, rows_ref.shape[2])
        lanes = slice(i * TILE, (i + 1) * TILE)
        rows_ref[:, 0, :, lanes] = jnp.where(first, own, other)
        rows_ref[:, 1, :, lanes] = jnp.where(first, other, own)
    product(k, rows_ref, weight_ref, outs)


def cost(weights):
    _, chips, share, depth = weights.shape
    return pl.CostEstimate(
        flops=2 * chips * share * depth * TILES * TILE,
        bytes_accessed=2 * chips * share * depth,
        transcendentals=0,
    )


def packed(weights, pieces, dtype):
    height = weights.shape[1] * weights.shape[2]
    return [jax.ShapeDtypeStruct(((2 * WHOLE + 1) * height // 2 // pieces, TILE), dtype)] * pieces


def join(k, place, own, other, weights):
    _, chips, _, depth = weights.shape
    rows = (chips, CORES, depth // (chips * CORES), TILES * TILE)
    rows, *outs = pl.pallas_call(
        functools.partial(join_kernel, k),
        out_shape=[jax.ShapeDtypeStruct(rows, BF16)] + packed(weights, PIECES[k], BF16),
        in_specs=[SMEM] + [VMEM] * 3,
        out_specs=[VMEM] * (1 + PIECES[k]),
        compiler_params=LIMIT,
        cost_estimate=cost(weights),
    )(place, own, other, weights)
    return outs, rows


def matmul_kernel(k, rows_ref, weight_ref, *outs):
    product(k, rows_ref, weight_ref, outs)


def matmul(k, rows, weights):
    return pl.pallas_call(
        functools.partial(matmul_kernel, k),
        out_shape=packed(weights, PIECES[k], BF16 if k else F32),
        in_specs=[VMEM] * 2,
        out_specs=[VMEM] * PIECES[k],
        compiler_params=LIMIT,
        cost_estimate=cost(weights),
    )(rows, weights)


def add_kernel(total_ref, *refs):
    gots, out_ref = refs[:-1], refs[-1]
    size = gots[0].shape[0]
    for i, got in enumerate(gots):
        here = slice(i * size, (i + 1) * size)
        out_ref[here] = total_ref[here] + got[...].astype(F32)


def add_last_kernel(total_ref, *refs):
    gots, out_ref = refs[:-1], refs[-1]
    size, height = gots[0].shape[0], out_ref.shape[0]
    whole = jnp.concatenate([got[...].astype(F32) for got in gots], axis=0) + total_ref[...]
    for place in range(WHOLE):
        part = whole[place * height : (place + 1) * height]
        out_ref[:, place * TILE : (place + 1) * TILE] = part.astype(BF16)
    part = whole[WHOLE * height :]
    part = jnp.concatenate([part, swap_halves(part)], axis=0)
    out_ref[:, WHOLE * TILE :] = part.astype(BF16)


def add(total, gots, last=False):
    height = 2 * total.shape[0] // (2 * WHOLE + 1)
    shape = jax.ShapeDtypeStruct((height, TILES * TILE), BF16)
    return pl.pallas_call(
        add_last_kernel if last else add_kernel,
        out_shape=shape if last else jax.ShapeDtypeStruct(total.shape, F32),
        in_specs=[VMEM] * (1 + len(gots)),
        out_specs=VMEM,
        compiler_params=LIMIT,
        cost_estimate=pl.CostEstimate(
            flops=total.size, bytes_accessed=10 * total.size, transcendentals=0
        ),
    )(total, *gots)


def update_kernel(plan, ladder_ref, rest_ref, occupied_ref, virtual_ref, out_ref):
    virtual_sum = virtual_ref[...]
    low = lax.broadcasted_iota(jnp.int32, (ladder_ref.shape[1], TILE), 1) < HALF
    half = slice(WHOLE * TILE, (WHOLE + 1) * TILE)
    for tile, (whole, halves) in enumerate(plan.sources()):
        lanes = slice(tile * TILE, (tile + 1) * TILE)
        if whole is not None:
            h, place = whole
            ladder = ladder_ref[h, :, place * TILE : (place + 1) * TILE].astype(F32)
        else:
            left, right = (ladder_ref[h, :, half].astype(F32) for h in halves)
            ladder = jnp.where(low, left, swap_halves(right))
        denominator = occupied_ref[:, lanes] - virtual_sum
        total = ladder + rest_ref[:, lanes].astype(F32)
        out_ref[:, lanes] = (total / denominator).astype(BF16)


def update(plan, ladder, rest, occupied_sum, virtual_sum):
    return pl.pallas_call(
        functools.partial(update_kernel, plan),
        out_shape=jax.ShapeDtypeStruct(rest.shape, BF16),
        compiler_params=LIMIT,
    )(ladder, rest, occupied_sum, virtual_sum)


def energy_sums(occupied, virtual, slab_start, pair_count, share):
    occupied_sum = (occupied[:, None] + occupied[None, :]).reshape(-1)[:pair_count]
    place = (lax.axis_index("z") * Y + lax.axis_index("y")) * CORES + lax.axis_index("core")
    row_base = (place * REPS + lax.axis_index("rep")) * share
    count = virtual.shape[0]
    pair_index = slab_start[0] + row_base + jnp.arange(share, dtype=jnp.int32)
    ids = jnp.arange(count, dtype=jnp.int32)
    pick_first = (pair_index // count)[:, None] == ids[None, :]
    pick_second = (pair_index % count)[:, None] == ids[None, :]
    zero = F32(0.0)
    first = jnp.sum(jnp.where(pick_first, virtual[None, :], zero), axis=1)
    second = jnp.sum(jnp.where(pick_second, virtual[None, :], zero), axis=1)
    return occupied_sum[None, :], (first + second)[:, None]


def shifted(array, axis, size, shift):
    return lax.ppermute(array, axis, [(i, (i + shift) % size) for i in range(size)])


def after(array, others):
    return lax.optimization_barrier((array, *others))[0]


def over_rep(place, own, other, weights):
    sent, rows = join(ORDER[0], place, own, other, weights)
    got = []
    for k in ORDER:
        blocks = sent if k == ORDER[0] else matmul(k, rows, weights)
        got.append([shifted(block, "rep", REPS, k) for block in blocks])
    total = matmul(0, rows, weights)[0]
    for blocks in got[:-1]:
        total = add(total, blocks)
    return add(total, got[-1], last=True)


def on_device(amplitudes, integrals, rest_terms, occupied_energy, virtual_energy, slab_start):
    amp = amplitudes[:, 0, :].T
    share, pair_count = rest_terms.shape
    plan = Plan(pair_count // TILE)
    occupied_sum, virtual_sum = energy_sums(
        occupied_energy, virtual_energy, slab_start, pair_count, share
    )
    place = jnp.stack([lax.axis_index(a) for a in ("z", "y", "core", "rep")]).astype(jnp.int32)
    split = integrals.reshape(CHIPS, CORES, REPS, share, integrals.shape[2])

    sent, place = lax.optimization_barrier((repack(plan, amp), place))
    own = lax.all_to_all(sent, ("z", "y"), split_axis=0, concat_axis=0, tiled=True)
    other = shifted(own, "core", CORES, 1)
    weights = hold(place, split, own)
    total = over_rep(place, own, other, weights)
    ladder = lax.all_to_all(
        total.reshape(CHIPS, share, -1), ("z", "y"), split_axis=0, concat_axis=0, tiled=True
    )
    return update(plan, ladder, rest_terms, occupied_sum, virtual_sum)


def solution(mesh):
    axes = ("z", "y", "core", "rep")
    split = Mesh(mesh.devices.reshape(Z, Y, CORES, REPS), axes)
    grid = axes[:3]
    placed = (P(None, "rep", grid), P(None, "rep", None), P(axes, None), P(), P(), P())
    return jax.shard_map(
        on_device, mesh=split, in_specs=placed, out_specs=P(axes, None), check_vma=False
    )
```

```python
import functools

import jax
import jax.numpy as jnp
from jax import lax
from jax.experimental import pallas as pl
from jax.experimental.pallas import tpu as pltpu
from jax.sharding import Mesh, PartitionSpec as P

Z, Y, CORES, REPS = 8, 4, 2, 4
CHIPS = Z * Y
TILE, HALF = 128, 64
WHOLE = 5
TILES = WHOLE + 1
STEP = 2 * TILE
ORDER = (1, 2, 3)
PIECES = (1, 1, 2, 1)
BF16, F32 = jnp.bfloat16, jnp.float32
ANY = pl.BlockSpec(memory_space=pl.ANY)
VMEM = pl.BlockSpec(memory_space=pltpu.VMEM)
SMEM = pl.BlockSpec(memory_space=pltpu.SMEM)
LIMIT = pltpu.CompilerParams(vmem_limit_bytes=24 * 1024 * 1024)


class Plan:
    def __init__(self, tiles):
        self.tiles = tiles
        halves, share = 2 * tiles, 2 * WHOLE + 1
        starts = [min(halves * h // CHIPS, halves - share) for h in range(CHIPS)]
        self.odd = [start % 2 for start in starts]
        self.first = [start // 2 + start % 2 for start in starts]
        self.split = [start // 2 if start % 2 else start // 2 + WHOLE for start in starts]

    def sources(self):
        whole, half = {}, {}
        for h in range(CHIPS):
            for place in range(WHOLE):
                whole.setdefault(self.first[h] + place, (h, place))
            half[self.split[h], self.odd[h]] = h
        return [
            (whole[tile], None) if tile in whole else (None, (half[tile, 0], half[tile, 1]))
            for tile in range(self.tiles)
        ]


def swap_halves(block):
    return jnp.concatenate([block[:, HALF:], block[:, :HALF]], axis=1)


def repack_kernel(plan, amp_ref, out_ref):
    depth = amp_ref.shape[0]
    middle = depth // 2
    low = lax.broadcasted_iota(jnp.int32, (middle, TILE), 1) < HALF
    for h in range(CHIPS):
        for place in range(WHOLE):
            start = (plan.first[h] + place) * TILE
            out_ref[h, place * depth : (place + 1) * depth] = amp_ref[:, start : start + TILE]
        block = amp_ref[:, plan.split[h] * TILE : (plan.split[h] + 1) * TILE].astype(F32)
        other = swap_halves(block)
        if plan.odd[h]:
            block, other = other, block
        packed = jnp.where(low, block[:middle], other[middle:])
        out_ref[h, WHOLE * depth :] = packed.astype(BF16)


def repack(plan, amp):
    depth = amp.shape[0]
    return pl.pallas_call(
        functools.partial(repack_kernel, plan),
        out_shape=jax.ShapeDtypeStruct((CHIPS, WHOLE * depth + depth // 2, TILE), BF16),
        in_specs=[VMEM],
        out_specs=VMEM,
        compiler_params=LIMIT,
    )(amp)


def hold_kernel(place_ref, weight_ref, _, out_ref, sem):
    core, rep = place_ref[2], place_ref[3]
    copies = [
        pltpu.make_async_copy(
            weight_ref.at[:, core, lax.rem(rep + k, REPS)], out_ref.at[k], sem.at[k]
        )
        for k in range(REPS)
    ]
    for copy in copies:
        copy.start()
    for copy in copies:
        copy.wait()


def hold(place, weights, own):
    chips, _, _, share, depth = weights.shape
    return pl.pallas_call(
        hold_kernel,
        out_shape=jax.ShapeDtypeStruct((REPS, chips, share, depth), BF16),
        in_specs=[SMEM, ANY, ANY],
        out_specs=VMEM,
        scratch_shapes=[pltpu.SemaphoreType.DMA((REPS,))],
        compiler_params=LIMIT,
    )(place, pltpu.with_memory_space_constraint(weights, pltpu.HBM), own)


def tile_of(ref, place, depth):
    if place < WHOLE:
        return ref[:, place * depth : (place + 1) * depth]
    packed = ref[:, WHOLE * depth :].astype(F32)
    swapped = jnp.concatenate([packed[:, :, HALF:], packed[:, :, :HALF]], axis=2)
    return jnp.concatenate([packed, swapped], axis=1).astype(BF16)


def product(k, rows_ref, weight_ref, outs):
    _, chips, share, depth = weight_ref.shape
    height = chips * share
    left = weight_ref[k].reshape(height, depth)
    parts = []
    for start in range(0, TILES * TILE, STEP):
        right = rows_ref[:, :, :, start : start + STEP].reshape(depth, STEP)
        term = jnp.dot(left, right, preferred_element_type=F32)
        parts += [term[:, :TILE], term[:, TILE:]]
    low = lax.broadcasted_iota(jnp.int32, (height // 2, TILE), 1) < HALF
    last = parts.pop()
    parts.append(jnp.where(low, last[: height // 2], swap_halves(last[height // 2 :])))
    at, end = 0, outs[0].shape[0]
    place = 0
    for part in parts:
        part = part.astype(outs[0].dtype)
        done = 0
        while done < part.shape[0]:
            size = min(part.shape[0] - done, end - at)
            outs[place][at : at + size] = part[done : done + size]
            at, done = at + size, done + size
            if at == end:
                place, at = place + 1, 0


def join_kernel(k, place_ref, own_ref, other_ref, weight_ref, rows_ref, *outs):
    first = place_ref[2] == 0
    for i in range(TILES):
        own = tile_of(own_ref, i, rows_ref.shape[2])
        other = tile_of(other_ref, i, rows_ref.shape[2])
        lanes = slice(i * TILE, (i + 1) * TILE)
        rows_ref[:, 0, :, lanes] = jnp.where(first, own, other)
        rows_ref[:, 1, :, lanes] = jnp.where(first, other, own)
    product(k, rows_ref, weight_ref, outs)


def cost(weights):
    _, chips, share, depth = weights.shape
    return pl.CostEstimate(
        flops=2 * chips * share * depth * TILES * TILE,
        bytes_accessed=2 * chips * share * depth,
        transcendentals=0,
    )


def packed(weights, pieces, dtype):
    height = weights.shape[1] * weights.shape[2]
    return [jax.ShapeDtypeStruct(((2 * WHOLE + 1) * height // 2 // pieces, TILE), dtype)] * pieces


def join(k, place, own, other, weights):
    _, chips, _, depth = weights.shape
    rows = (chips, CORES, depth // (chips * CORES), TILES * TILE)
    rows, *outs = pl.pallas_call(
        functools.partial(join_kernel, k),
        out_shape=[jax.ShapeDtypeStruct(rows, BF16)] + packed(weights, PIECES[k], BF16),
        in_specs=[SMEM] + [VMEM] * 3,
        out_specs=[VMEM] * (1 + PIECES[k]),
        compiler_params=LIMIT,
        cost_estimate=cost(weights),
    )(place, own, other, weights)
    return outs, rows


def matmul_kernel(k, rows_ref, weight_ref, *outs):
    product(k, rows_ref, weight_ref, outs)


def matmul(k, rows, weights):
    return pl.pallas_call(
        functools.partial(matmul_kernel, k),
        out_shape=packed(weights, PIECES[k], BF16 if k else F32),
        in_specs=[VMEM] * 2,
        out_specs=[VMEM] * PIECES[k],
        compiler_params=LIMIT,
        cost_estimate=cost(weights),
    )(rows, weights)


def add_kernel(total_ref, *refs):
    gots, out_ref = refs[:-1], refs[-1]
    size = gots[0].shape[0]
    for i, got in enumerate(gots):
        here = slice(i * size, (i + 1) * size)
        out_ref[here] = total_ref[here] + got[...].astype(F32)


def add_last_kernel(total_ref, *refs):
    gots, out_ref = refs[:-1], refs[-1]
    size, height = gots[0].shape[0], out_ref.shape[0]
    whole = jnp.concatenate([got[...].astype(F32) for got in gots], axis=0) + total_ref[...]
    for place in range(WHOLE):
        part = whole[place * height : (place + 1) * height]
        out_ref[:, place * TILE : (place + 1) * TILE] = part.astype(BF16)
    part = whole[WHOLE * height :]
    part = jnp.concatenate([part, swap_halves(part)], axis=0)
    out_ref[:, WHOLE * TILE :] = part.astype(BF16)


def add(total, gots, last=False):
    height = 2 * total.shape[0] // (2 * WHOLE + 1)
    shape = jax.ShapeDtypeStruct((height, TILES * TILE), BF16)
    return pl.pallas_call(
        add_last_kernel if last else add_kernel,
        out_shape=shape if last else jax.ShapeDtypeStruct(total.shape, F32),
        in_specs=[VMEM] * (1 + len(gots)),
        out_specs=VMEM,
        compiler_params=LIMIT,
        cost_estimate=pl.CostEstimate(
            flops=total.size, bytes_accessed=10 * total.size, transcendentals=0
        ),
    )(total, *gots)


def update_kernel(plan, ladder_ref, rest_ref, occupied_ref, virtual_ref, out_ref):
    virtual_sum = virtual_ref[...]
    low = lax.broadcasted_iota(jnp.int32, (ladder_ref.shape[1], TILE), 1) < HALF
    half = slice(WHOLE * TILE, (WHOLE + 1) * TILE)
    for tile, (whole, halves) in enumerate(plan.sources()):
        lanes = slice(tile * TILE, (tile + 1) * TILE)
        if whole is not None:
            h, place = whole
            ladder = ladder_ref[h, :, place * TILE : (place + 1) * TILE].astype(F32)
        else:
            left, right = (ladder_ref[h, :, half].astype(F32) for h in halves)
            ladder = jnp.where(low, left, swap_halves(right))
        denominator = occupied_ref[:, lanes] - virtual_sum
        total = ladder + rest_ref[:, lanes].astype(F32)
        out_ref[:, lanes] = (total / denominator).astype(BF16)


def update(plan, ladder, rest, occupied_sum, virtual_sum):
    return pl.pallas_call(
        functools.partial(update_kernel, plan),
        out_shape=jax.ShapeDtypeStruct(rest.shape, BF16),
        compiler_params=LIMIT,
    )(ladder, rest, occupied_sum, virtual_sum)


def energy_sums(occupied, virtual, slab_start, pair_count, share):
    occupied_sum = (occupied[:, None] + occupied[None, :]).reshape(-1)[:pair_count]
    place = (lax.axis_index("z") * Y + lax.axis_index("y")) * CORES + lax.axis_index("core")
    row_base = (place * REPS + lax.axis_index("rep")) * share
    count = virtual.shape[0]
    pair_index = slab_start[0] + row_base + jnp.arange(share, dtype=jnp.int32)
    ids = jnp.arange(count, dtype=jnp.int32)
    pick_first = (pair_index // count)[:, None] == ids[None, :]
    pick_second = (pair_index % count)[:, None] == ids[None, :]
    zero = F32(0.0)
    first = jnp.sum(jnp.where(pick_first, virtual[None, :], zero), axis=1)
    second = jnp.sum(jnp.where(pick_second, virtual[None, :], zero), axis=1)
    return occupied_sum[None, :], (first + second)[:, None]


def shifted(array, axis, size, shift):
    return lax.ppermute(array, axis, [(i, (i + shift) % size) for i in range(size)])


def after(array, others):
    return lax.optimization_barrier((array, *others))[0]


def over_rep(place, own, other, weights):
    sent, rows = join(ORDER[0], place, own, other, weights)
    got = []
    for k in ORDER:
        blocks = sent if k == ORDER[0] else matmul(k, rows, weights)
        got.append([shifted(block, "rep", REPS, k) for block in blocks])
    total = matmul(0, rows, weights)[0]
    for blocks in got[:-1]:
        total = add(total, blocks)
    return add(total, got[-1], last=True)


def on_device(amplitudes, integrals, rest_terms, occupied_energy, virtual_energy, slab_start):
    amp = amplitudes[:, 0, :].T
    share, pair_count = rest_terms.shape
    plan = Plan(pair_count // TILE)
    occupied_sum, virtual_sum = energy_sums(
        occupied_energy, virtual_energy, slab_start, pair_count, share
    )
    place = jnp.stack([lax.axis_index(a) for a in ("z", "y", "core", "rep")]).astype(jnp.int32)
    split = integrals.reshape(CHIPS, CORES, REPS, share, integrals.shape[2])

    sent, place = lax.optimization_barrier((repack(plan, amp), place))
    own = lax.all_to_all(sent, ("z", "y"), split_axis=0, concat_axis=0, tiled=True)
    other = shifted(own, "core", CORES, 1)
    weights = hold(place, split, own)
    total = over_rep(place, own, other, weights)
    ladder = lax.all_to_all(
        total.reshape(CHIPS, share, -1), ("z", "y"), split_axis=0, concat_axis=0, tiled=True
    )
    return update(plan, ladder, rest_terms, occupied_sum, virtual_sum)


def solution(mesh):
    axes = ("z", "y", "core", "rep")
    split = Mesh(mesh.devices.reshape(Z, Y, CORES, REPS), axes)
    grid = axes[:3]
    placed = (P(None, "rep", grid), P(None, "rep", None), P(axes, None), P(), P(), P())
    return jax.shard_map(
        on_device, mesh=split, in_specs=placed, out_specs=P(axes, None), check_vma=False
    )
```

```python
import functools

import jax
import jax.numpy as jnp
from jax import lax
from jax.experimental import pallas as pl
from jax.experimental.pallas import tpu as pltpu
from jax.sharding import Mesh, PartitionSpec as P

Z, Y, CORES, REPS = 8, 4, 2, 4
CHIPS = Z * Y
TILE, HALF = 128, 64
WHOLE = 5
TILES = WHOLE + 1
STEP = 2 * TILE
ORDER = (1, 2, 3)
PIECES = (1, 1, 1, 1)
BF16, F32 = jnp.bfloat16, jnp.float32
ANY = pl.BlockSpec(memory_space=pl.ANY)
VMEM = pl.BlockSpec(memory_space=pltpu.VMEM)
SMEM = pl.BlockSpec(memory_space=pltpu.SMEM)
LIMIT = pltpu.CompilerParams(vmem_limit_bytes=24 * 1024 * 1024)


class Plan:
    def __init__(self, tiles):
        self.tiles = tiles
        halves, share = 2 * tiles, 2 * WHOLE + 1
        starts = [min(halves * h // CHIPS, halves - share) for h in range(CHIPS)]
        self.odd = [start % 2 for start in starts]
        self.first = [start // 2 + start % 2 for start in starts]
        self.split = [start // 2 if start % 2 else start // 2 + WHOLE for start in starts]

    def sources(self):
        whole, half = {}, {}
        for h in range(CHIPS):
            for place in range(WHOLE):
                whole.setdefault(self.first[h] + place, (h, place))
            half[self.split[h], self.odd[h]] = h
        return [
            (whole[tile], None) if tile in whole else (None, (half[tile, 0], half[tile, 1]))
            for tile in range(self.tiles)
        ]


def swap_halves(block):
    return jnp.concatenate([block[:, HALF:], block[:, :HALF]], axis=1)


def repack_kernel(plan, amp_ref, out_ref):
    depth = amp_ref.shape[0]
    middle = depth // 2
    low = lax.broadcasted_iota(jnp.int32, (middle, TILE), 1) < HALF
    for h in range(CHIPS):
        for place in range(WHOLE):
            start = (plan.first[h] + place) * TILE
            out_ref[h, place * depth : (place + 1) * depth] = amp_ref[:, start : start + TILE]
        block = amp_ref[:, plan.split[h] * TILE : (plan.split[h] + 1) * TILE].astype(F32)
        other = swap_halves(block)
        if plan.odd[h]:
            block, other = other, block
        packed = jnp.where(low, block[:middle], other[middle:])
        out_ref[h, WHOLE * depth :] = packed.astype(BF16)


def repack(plan, amp):
    depth = amp.shape[0]
    return pl.pallas_call(
        functools.partial(repack_kernel, plan),
        out_shape=jax.ShapeDtypeStruct((CHIPS, WHOLE * depth + depth // 2, TILE), BF16),
        in_specs=[VMEM],
        out_specs=VMEM,
        compiler_params=LIMIT,
    )(amp)


def hold_kernel(place_ref, weight_ref, _, out_ref, sem):
    core, rep = place_ref[2], place_ref[3]
    copies = [
        pltpu.make_async_copy(
            weight_ref.at[:, core, lax.rem(rep + k, REPS)], out_ref.at[k], sem.at[k]
        )
        for k in range(REPS)
    ]
    for copy in copies:
        copy.start()
    for copy in copies:
        copy.wait()


def hold(place, weights, own):
    chips, _, _, share, depth = weights.shape
    return pl.pallas_call(
        hold_kernel,
        out_shape=jax.ShapeDtypeStruct((REPS, chips, share, depth), BF16),
        in_specs=[SMEM, ANY, ANY],
        out_specs=VMEM,
        scratch_shapes=[pltpu.SemaphoreType.DMA((REPS,))],
        compiler_params=LIMIT,
    )(place, pltpu.with_memory_space_constraint(weights, pltpu.HBM), own)


def tile_of(ref, place, depth):
    if place < WHOLE:
        return ref[:, place * depth : (place + 1) * depth]
    packed = ref[:, WHOLE * depth :].astype(F32)
    swapped = jnp.concatenate([packed[:, :, HALF:], packed[:, :, :HALF]], axis=2)
    return jnp.concatenate([packed, swapped], axis=1).astype(BF16)


def product(k, rows_ref, weight_ref, outs):
    _, chips, share, depth = weight_ref.shape
    height = chips * share
    left = weight_ref[k].reshape(height, depth)
    parts = []
    for start in range(0, TILES * TILE, STEP):
        right = rows_ref[:, :, :, start : start + STEP].reshape(depth, STEP)
        term = jnp.dot(left, right, preferred_element_type=F32)
        parts += [term[:, :TILE], term[:, TILE:]]
    low = lax.broadcasted_iota(jnp.int32, (height // 2, TILE), 1) < HALF
    last = parts.pop()
    parts.append(jnp.where(low, last[: height // 2], swap_halves(last[height // 2 :])))
    at, end = 0, outs[0].shape[0]
    place = 0
    for part in parts:
        part = part.astype(outs[0].dtype)
        done = 0
        while done < part.shape[0]:
            size = min(part.shape[0] - done, end - at)
            outs[place][at : at + size] = part[done : done + size]
            at, done = at + size, done + size
            if at == end:
                place, at = place + 1, 0


def join_kernel(k, place_ref, own_ref, other_ref, weight_ref, rows_ref, *outs):
    first = place_ref[2] == 0
    for i in range(TILES):
        own = tile_of(own_ref, i, rows_ref.shape[2])
        other = tile_of(other_ref, i, rows_ref.shape[2])
        lanes = slice(i * TILE, (i + 1) * TILE)
        rows_ref[:, 0, :, lanes] = jnp.where(first, own, other)
        rows_ref[:, 1, :, lanes] = jnp.where(first, other, own)
    product(k, rows_ref, weight_ref, outs)


def cost(weights):
    _, chips, share, depth = weights.shape
    return pl.CostEstimate(
        flops=2 * chips * share * depth * TILES * TILE,
        bytes_accessed=2 * chips * share * depth,
        transcendentals=0,
    )


def packed(weights, pieces, dtype):
    height = weights.shape[1] * weights.shape[2]
    return [jax.ShapeDtypeStruct(((2 * WHOLE + 1) * height // 2 // pieces, TILE), dtype)] * pieces


def join(k, place, own, other, weights):
    _, chips, _, depth = weights.shape
    rows = (chips, CORES, depth // (chips * CORES), TILES * TILE)
    rows, *outs = pl.pallas_call(
        functools.partial(join_kernel, k),
        out_shape=[jax.ShapeDtypeStruct(rows, BF16)] + packed(weights, PIECES[k], BF16),
        in_specs=[SMEM] + [VMEM] * 3,
        out_specs=[VMEM] * (1 + PIECES[k]),
        compiler_params=LIMIT,
        cost_estimate=cost(weights),
    )(place, own, other, weights)
    return outs, rows


def matmul_kernel(k, rows_ref, weight_ref, *outs):
    product(k, rows_ref, weight_ref, outs)


def matmul(k, rows, weights):
    return pl.pallas_call(
        functools.partial(matmul_kernel, k),
        out_shape=packed(weights, PIECES[k], BF16 if k else F32),
        in_specs=[VMEM] * 2,
        out_specs=[VMEM] * PIECES[k],
        compiler_params=LIMIT,
        cost_estimate=cost(weights),
    )(rows, weights)


def add_kernel(total_ref, *refs):
    gots, out_ref = refs[:-1], refs[-1]
    size = gots[0].shape[0]
    for i, got in enumerate(gots):
        here = slice(i * size, (i + 1) * size)
        out_ref[here] = total_ref[here] + got[...].astype(F32)


def add_last_kernel(total_ref, *refs):
    gots, out_ref = refs[:-1], refs[-1]
    size, height = gots[0].shape[0], out_ref.shape[0]
    whole = jnp.concatenate([got[...].astype(F32) for got in gots], axis=0) + total_ref[...]
    for place in range(WHOLE):
        part = whole[place * height : (place + 1) * height]
        out_ref[:, place * TILE : (place + 1) * TILE] = part.astype(BF16)
    part = whole[WHOLE * height :]
    part = jnp.concatenate([part, swap_halves(part)], axis=0)
    out_ref[:, WHOLE * TILE :] = part.astype(BF16)


def add(total, gots, last=False):
    height = 2 * total.shape[0] // (2 * WHOLE + 1)
    shape = jax.ShapeDtypeStruct((height, TILES * TILE), BF16)
    return pl.pallas_call(
        add_last_kernel if last else add_kernel,
        out_shape=shape if last else jax.ShapeDtypeStruct(total.shape, F32),
        in_specs=[VMEM] * (1 + len(gots)),
        out_specs=VMEM,
        compiler_params=LIMIT,
        cost_estimate=pl.CostEstimate(
            flops=total.size, bytes_accessed=10 * total.size, transcendentals=0
        ),
    )(total, *gots)


def update_kernel(plan, ladder_ref, rest_ref, occupied_ref, virtual_ref, out_ref):
    virtual_sum = virtual_ref[...]
    low = lax.broadcasted_iota(jnp.int32, (ladder_ref.shape[1], TILE), 1) < HALF
    half = slice(WHOLE * TILE, (WHOLE + 1) * TILE)
    for tile, (whole, halves) in enumerate(plan.sources()):
        lanes = slice(tile * TILE, (tile + 1) * TILE)
        if whole is not None:
            h, place = whole
            ladder = ladder_ref[h, :, place * TILE : (place + 1) * TILE].astype(F32)
        else:
            left, right = (ladder_ref[h, :, half].astype(F32) for h in halves)
            ladder = jnp.where(low, left, swap_halves(right))
        denominator = occupied_ref[:, lanes] - virtual_sum
        total = ladder + rest_ref[:, lanes].astype(F32)
        out_ref[:, lanes] = (total / denominator).astype(BF16)


def update(plan, ladder, rest, occupied_sum, virtual_sum):
    return pl.pallas_call(
        functools.partial(update_kernel, plan),
        out_shape=jax.ShapeDtypeStruct(rest.shape, BF16),
        compiler_params=LIMIT,
    )(ladder, rest, occupied_sum, virtual_sum)


def energy_sums(occupied, virtual, slab_start, pair_count, share):
    occupied_sum = (occupied[:, None] + occupied[None, :]).reshape(-1)[:pair_count]
    place = (lax.axis_index("z") * Y + lax.axis_index("y")) * CORES + lax.axis_index("core")
    row_base = (place * REPS + lax.axis_index("rep")) * share
    count = virtual.shape[0]
    pair_index = slab_start[0] + row_base + jnp.arange(share, dtype=jnp.int32)
    ids = jnp.arange(count, dtype=jnp.int32)
    pick_first = (pair_index // count)[:, None] == ids[None, :]
    pick_second = (pair_index % count)[:, None] == ids[None, :]
    zero = F32(0.0)
    first = jnp.sum(jnp.where(pick_first, virtual[None, :], zero), axis=1)
    second = jnp.sum(jnp.where(pick_second, virtual[None, :], zero), axis=1)
    return occupied_sum[None, :], (first + second)[:, None]


def shifted(array, axis, size, shift):
    return lax.ppermute(array, axis, [(i, (i + shift) % size) for i in range(size)])


def after(array, others):
    return lax.optimization_barrier((array, *others))[0]


def over_rep(place, own, other, weights):
    sent, rows = join(ORDER[0], place, own, other, weights)
    got = []
    for k in ORDER:
        blocks = sent if k == ORDER[0] else matmul(k, rows, weights)
        got.append([shifted(block, "rep", REPS, k) for block in blocks])
    total = matmul(0, rows, weights)[0]
    for blocks in (got[1], got[0]):
        total = add(total, blocks)
    return add(total, got[-1], last=True)


def on_device(amplitudes, integrals, rest_terms, occupied_energy, virtual_energy, slab_start):
    amp = amplitudes[:, 0, :].T
    share, pair_count = rest_terms.shape
    plan = Plan(pair_count // TILE)
    occupied_sum, virtual_sum = energy_sums(
        occupied_energy, virtual_energy, slab_start, pair_count, share
    )
    place = jnp.stack([lax.axis_index(a) for a in ("z", "y", "core", "rep")]).astype(jnp.int32)
    split = integrals.reshape(CHIPS, CORES, REPS, share, integrals.shape[2])

    sent, place = lax.optimization_barrier((repack(plan, amp), place))
    own = lax.all_to_all(sent, ("z", "y"), split_axis=0, concat_axis=0, tiled=True)
    other = shifted(own, "core", CORES, 1)
    weights = hold(place, split, own)
    total = over_rep(place, own, other, weights)
    ladder = lax.all_to_all(
        total.reshape(CHIPS, share, -1), ("z", "y"), split_axis=0, concat_axis=0, tiled=True
    )
    return update(plan, ladder, rest_terms, occupied_sum, virtual_sum)


def solution(mesh):
    axes = ("z", "y", "core", "rep")
    split = Mesh(mesh.devices.reshape(Z, Y, CORES, REPS), axes)
    grid = axes[:3]
    placed = (P(None, "rep", grid), P(None, "rep", None), P(axes, None), P(), P(), P())
    return jax.shard_map(
        on_device, mesh=split, in_specs=placed, out_specs=P(axes, None), check_vma=False
    )
```
